32 devices in a mesh: grp: 8 (over y, x, core), sl: 4 (over z).
Axes of the slice: x: 2, y: 2, z: 4, core: 2. Of those that a mesh axis runs over, the one named last changes fastest.
Arguments:
- tokens: bfloat16 [256, 3072], P('grp', 'sl'), may hold values from -6 to 6
- grad_out: bfloat16 [256, 3072], P('grp', 'sl'), may hold values from -6 to 6
- expert_ids: int32 [256, 2], P('grp'), may hold values from 0 to 7, all different within a row; in each aligned block of 32 rows (0 to 31, 32 to 63, ...) at most 16 rows name the same one
- gate_probs: float32 [256, 2], P('grp'), may hold values from 0.2 to 1
- gate_weight: bfloat16 [8, 18432, 3072], P('grp', 'sl'), may hold values from -0.109375 to 0.109375
- up_weight: bfloat16 [8, 18432, 3072], P('grp', 'sl'), may hold values from -0.109375 to 0.109375
- down_weight: bfloat16 [8, 18432, 3072], P('grp', 'sl'), may hold values from -0.046875 to 0.046875
Outputs:
- grad_input: bfloat16 [256, 3072], P('grp', 'sl')
- grad_down: bfloat16 [8, 18432, 3072], P('grp', 'sl')
The draws below stay inside these ranges and needn't reach their ends.
Inputs may be any that keep to these rules, and one draw needn't show every extreme that they name: `expert_ids`: each token names two different experts. Among the 32 tokens of one group no expert is named more than 16 times, a bound that some block reaches.
All inputs are finite; a program needn't handle non-finite values.
Results may differ from the reference program's by a relative error of at most 0.0057.
Values may be sent and summed in bfloat16 or wider, within the bound.
A program may use at most 256 MiB of HBM per device.

```python
import math
import jax
import jax.numpy as jnp
import numpy as np
from jax import lax

D = 3072
FF = 18432
EXPERTS = 8
TOK_G = 32
CAP = 16
OWNERS = 1
TOKENS = 256
N_GRP = 8


def levels(own_key, extent, cuts, smallest, largest):
    def one(axis_at, blocks):
        draws = jax.random.uniform(jax.random.fold_in(jax.random.fold_in(own_key, 6), axis_at), (blocks,), jnp.float32, smallest / len(cuts), largest / len(cuts))
        return jnp.repeat(jnp.exp(draws), extent[axis_at] // blocks).reshape((-1,) + (1,) * (len(extent) - axis_at - 1))

    level = one(*cuts[0])
    for cut in cuts[1:]:
        level = level * one(*cut)
    return level


def routed_block(rng, own, number, rows, amount, top, limit, skew):
    ranking = jax.random.permutation(rng, amount)
    heavy_load, common = shares(amount, rows * top, limit, skew, True), shares(amount, rows * top, limit, skew, False)
    places = jnp.arange(amount)

    def named(tallies, rotation):
        used = int((tallies > 0).sum())
        fixed = max(1, used // 4)
        shifted = fixed + (places - fixed + rotation * (used - fixed)) % max(1, amount - fixed)
        return jnp.zeros((amount,), jnp.int32).at[ranking[jnp.where(places < fixed, places, shifted)]].set(jnp.asarray(tallies, jnp.int32))

    tallies = jnp.where(number % 4 == 0, named(heavy_load, number // 4), named(common, number - number // 4 - 1))
    mixed = jax.random.permutation(jax.random.fold_in(own, 3), amount)
    source_of, taker = mixed[0:amount // 2 * 2:2], mixed[1:amount // 2 * 2:2]
    margin = jnp.minimum(tallies[source_of] - 1, limit - tallies[taker]) // 2
    margin = jnp.where((source_of == ranking[0]) | (taker == ranking[0]) | (tallies[taker] == 0), 0, jnp.maximum(margin, 0))
    shifted = jax.random.randint(jax.random.fold_in(own, 4), (amount // 2,), 0, 1 << 20) % (margin + 1)
    tallies = tallies.at[source_of].add(-shifted).at[taker].add(shifted)
    members = jnp.searchsorted(jnp.cumsum(tallies), jnp.arange(rows * top), side="right").astype(jnp.int32)
    grid = members.reshape(top, rows).T
    grid = grid[jax.random.permutation(jax.random.fold_in(own, 1), rows)]
    rotation = jax.random.randint(jax.random.fold_in(own, 2), (rows, 1), 0, top)
    return jnp.take_along_axis(grid, (jnp.arange(top)[None, :] + rotation) % top, axis=1)


def shares(count, total, reach, skew, full):
    weights = [(1 << 20) // math.isqrt(standing ** skew) + 1 for standing in range(1, count + 1)]
    largest = reach if full else min(reach, max(-(-total // count), total * weights[0] // sum(weights)))
    least = 1 if total - largest >= count - 1 else 0
    holding, spare = [largest] + [least] * (count - 1), total - largest - least * (count - 1)
    while spare > 0:
        candidates = [i for i in range(1, count) if holding[i] < largest] or [i for i in range(1, count) if holding[i] < reach]
        mass, remaining = sum([weights[i] for i in candidates]), spare
        for i in candidates:
            extra = min(reach - holding[i], max(1, remaining * weights[i] // mass), spare)
            holding[i] = holding[i] + extra
            spare = spare - extra
    return np.array(holding)


def centred(rng, shape, scale, limit, split=(), kind=jnp.bfloat16):
    factor_of = levels(rng, shape, split, -0.22, 0.18) if split else 1.0
    entries = jax.random.normal(rng, shape, jnp.float32) * scale * factor_of
    return jnp.minimum(jnp.maximum(entries, -limit), limit).astype(kind)


def setup_inputs(seed: int = 0) -> dict:
    keys = jax.random.split(jax.random.key(seed), 8)
    tokens = centred(keys[0], (TOKENS, D), 1.0, 6.0, ((0, 8), (1, 4)))
    grad_out = centred(keys[1], (TOKENS, D), 1.0, 6.0, ((0, 8), (1, 4)))
    expert_ids_keys = jax.random.split(jax.random.fold_in(keys[2], 1), TOKENS // TOK_G)
    expert_ids_turns = jax.random.permutation(jax.random.fold_in(keys[2], 3), TOKENS // TOK_G)
    expert_ids = jax.vmap(lambda own, number: routed_block(jax.random.fold_in(keys[2], 2), own, number, TOK_G, EXPERTS, 2, CAP, 2))(expert_ids_keys, expert_ids_turns).reshape((TOKENS, 2))
    gate_probs = jnp.clip(0.2 + 0.8 * jax.random.uniform(keys[3], (TOKENS, 2), jnp.float32) ** levels(keys[3], (TOKENS, 2), ((0, 8),), -0.2, 0.2), 0.2, 1.0)
    gate_weight = centred(keys[4], (EXPERTS * OWNERS, FF // OWNERS, D), D ** -0.5, 0.109375, ((0, 8), (1, 4)))
    up_weight = centred(keys[5], (EXPERTS * OWNERS, FF // OWNERS, D), D ** -0.5, 0.109375, ((0, 8), (1, 4)))
    down_weight = centred(keys[6], (EXPERTS * OWNERS, FF // OWNERS, D), FF ** -0.5, 0.046875, ((0, 8), (1, 4)))
    return dict(tokens=tokens, grad_out=grad_out, expert_ids=expert_ids, gate_probs=gate_probs, gate_weight=gate_weight, up_weight=up_weight, down_weight=down_weight)


def slot_table(group_ids, capacity):
    flat_ids = group_ids.reshape(-1)
    expert_list = jnp.arange(EXPERTS, dtype=jnp.int32)
    onehot = (flat_ids[:, None] == expert_list[None, :]).astype(jnp.int32)
    earlier = jnp.cumsum(onehot, axis=0) - onehot
    slot_of = jnp.sum(earlier * onehot, axis=1).astype(jnp.int32)
    expert_hit = flat_ids[None, None, :] == expert_list[:, None, None]
    slot_hit = slot_of[None, None, :] == jnp.arange(capacity, dtype=jnp.int32)[None, :, None]
    return jnp.logical_and(expert_hit, slot_hit).astype(jnp.bfloat16)


def expert_grads(items):
    gate_local, up_local, down_local, rows_in, rows_grad = items
    contract_feat = (((1,), (1,)), ((), ()))
    contract_rows = (((0,), (0,)), ((), ()))
    gate_acts = lax.dot_general(rows_in, gate_local, contract_feat, preferred_element_type=jnp.float32)
    up_acts = lax.dot_general(rows_in, up_local, contract_feat, preferred_element_type=jnp.float32)
    sigmoid_g = jax.nn.sigmoid(gate_acts)
    silu_g = gate_acts * sigmoid_g
    hidden = (silu_g * up_acts).astype(jnp.bfloat16)
    grad_hidden = lax.dot_general(rows_grad, down_local, contract_feat, preferred_element_type=jnp.float32)
    grad_down = lax.dot_general(hidden, rows_grad, contract_rows, preferred_element_type=jnp.float32).astype(jnp.bfloat16)
    grad_gate = (grad_hidden * up_acts * sigmoid_g * (1.0 + gate_acts * (1.0 - sigmoid_g))).astype(jnp.bfloat16)
    grad_up = (grad_hidden * silu_g).astype(jnp.bfloat16)
    partial_value = jnp.dot(grad_gate, gate_local, preferred_element_type=jnp.float32) + jnp.dot(grad_up, up_local, preferred_element_type=jnp.float32)
    return grad_down, partial_value


def reference(tokens, grad_out, expert_ids, gate_probs, gate_weight, up_weight, down_weight):
    selector = jax.vmap(lambda group_ids: slot_table(group_ids, CAP))(expert_ids.reshape(N_GRP, TOK_G, 2))
    selector_f = selector.astype(jnp.float32)
    token_rows = jnp.repeat(tokens.reshape(N_GRP, TOK_G, D), 2, axis=1)
    grad_rows = jnp.repeat(grad_out.reshape(N_GRP, TOK_G, D), 2, axis=1).astype(jnp.float32)
    scaled = (gate_probs.reshape(N_GRP, 2 * TOK_G, 1) * grad_rows).astype(jnp.bfloat16)
    packed_in = jnp.einsum("geca,gad->egcd", selector_f, token_rows.astype(jnp.float32)).astype(jnp.bfloat16)
    packed_grad = jnp.einsum("geca,gad->egcd", selector_f, scaled.astype(jnp.float32)).astype(jnp.bfloat16)
    packed_in = packed_in.reshape(EXPERTS, N_GRP * CAP, D)
    packed_grad = packed_grad.reshape(EXPERTS, N_GRP * CAP, D)
    gate_all = gate_weight.reshape(EXPERTS, FF, D)
    up_all = up_weight.reshape(EXPERTS, FF, D)
    down_all = down_weight.reshape(EXPERTS, FF, D)
    grad_down, partials = lax.map(expert_grads, (gate_all, up_all, down_all, packed_in, packed_grad))
    partials = partials.reshape(EXPERTS, N_GRP, CAP, D)
    per_assign = jnp.einsum("geca,egcd->gad", selector_f, partials, precision=lax.Precision.HIGHEST)
    grad_input = per_assign.reshape(N_GRP, TOK_G, 2, D).sum(axis=2).astype(jnp.bfloat16).reshape(TOKENS, D)
    return grad_input, grad_down.reshape(EXPERTS * OWNERS, FF // OWNERS, D)
```

```python
import functools

import jax
import jax.numpy as jnp
from jax import lax
from jax.experimental import pallas as pl
from jax.experimental.pallas import tpu as pltpu
from jax.sharding import PartitionSpec as P

EXPERTS = 8
MESH = pl.DeviceIdType.MESH
BIG = 56 * 1024 * 1024


def greet(n_g, n_s):
    g, s = lax.axis_index("grp"), lax.axis_index("sl")
    barrier = pltpu.get_barrier_semaphore()

    @pl.loop(1, n_g)
    def _(j):
        pl.semaphore_signal(
            barrier, inc=1, device_id=(lax.rem(g + j, n_g), s), device_id_type=MESH
        )

    @pl.loop(1, n_s)
    def _(j):
        pl.semaphore_signal(
            barrier, inc=1, device_id=(g, lax.rem(s + j, n_s)), device_id_type=MESH
        )

    pl.semaphore_wait(barrier, n_g - 1 + n_s - 1)


def slots(ids_ref):
    count = ids_ref.shape[0]
    first, second = ids_ref[:, 0:1], ids_ref[:, 1:2]
    lane = lax.broadcasted_iota(jnp.int32, (count, 128), 1)
    hit0 = (lane == first).astype(jnp.float32)
    hit1 = (lane == second).astype(jnp.float32)
    row = lax.broadcasted_iota(jnp.int32, (count, count), 0)
    col = lax.broadcasted_iota(jnp.int32, (count, count), 1)
    before = (col < row).astype(jnp.float32)
    earlier = jnp.dot(before, hit0 + hit1, preferred_element_type=jnp.float32)
    slot0 = jnp.sum(earlier * hit0, axis=1, keepdims=True).astype(jnp.int32)
    slot1 = jnp.sum(earlier * hit1, axis=1, keepdims=True).astype(jnp.int32)
    return first, second, slot0, slot1


def pick(expert, slot, cap, owners, width):
    lane = lax.broadcasted_iota(jnp.int32, (expert.shape[0], width), 1)
    table = jnp.zeros((expert.shape[0], width), jnp.float32)
    for owner in range(owners):
        table = table + (lane == (expert * owners + owner) * cap + slot).astype(jnp.float32)
    return table.astype(jnp.bfloat16)


def over_rows(left, right):
    return lax.dot_general(
        left, right, (((0,), (0,)), ((), ())), preferred_element_type=jnp.float32
    )


def dispatch_kernel(
    n_g, n_s, tok_ref, grad_ref, ids_ref, prob_ref, out_ref,
    raw, stage, table, send_a, recv_a, send_b, recv_b,
):
    g, s = lax.axis_index("grp"), lax.axis_index("sl")
    count, fc = tok_ref.shape
    cap = count // 2
    owners = n_g // EXPERTS
    greet(n_g, n_s)

    @pl.loop(1, n_s)
    def _(k):
        peer = lax.rem(s + k, n_s)
        for part, ref in enumerate((tok_ref, grad_ref)):
            pltpu.make_async_remote_copy(
                src_ref=ref, dst_ref=raw.at[s, part], send_sem=send_a, recv_sem=recv_a.at[s],
                device_id=(g, peer), device_id_type=MESH,
            ).start()

    first, second, slot0, slot1 = slots(ids_ref)
    table[0] = pick(first, slot0, cap, 1, EXPERTS * cap)
    table[1] = pick(second, slot1, cap, 1, EXPERTS * cap)

    def pack(src, tokens, grads):
        sel0, sel1 = table[0], table[1]
        wide = grads.astype(jnp.float32)
        scaled0 = (prob_ref[:, 0:1] * wide).astype(jnp.bfloat16)
        scaled1 = (prob_ref[:, 1:2] * wide).astype(jnp.bfloat16)
        stage[src, 0] = over_rows(sel0 + sel1, tokens).astype(jnp.bfloat16)
        stage[src, 1] = (over_rows(sel0, scaled0) + over_rows(sel1, scaled1)).astype(jnp.bfloat16)
        columns = pl.ds(pl.multiple_of(src * fc, 128), fc)
        mine = pl.ds(pl.multiple_of(g * cap, 16), cap)

        @pl.loop(1, n_g)
        def _(j):
            dest = lax.rem(g + j, n_g)
            theirs = pl.ds(pl.multiple_of((dest // owners) * cap, 16), cap)
            pltpu.make_async_remote_copy(
                src_ref=stage.at[src, :, theirs, :],
                dst_ref=out_ref.at[:, mine, columns],
                send_sem=send_b, recv_sem=recv_b,
                device_id=(dest, s), device_id_type=MESH,
            ).start()

        own = pl.ds(pl.multiple_of((g // owners) * cap, 16), cap)
        out_ref[0, mine, columns] = stage[src, 0, own, :]
        out_ref[1, mine, columns] = stage[src, 1, own, :]

    pack(s, tok_ref[...], grad_ref[...])

    @pl.loop(1, n_s)
    def _(k):
        src = lax.rem(s + k, n_s)
        pltpu.make_async_copy(raw.at[src], raw.at[src], recv_a.at[src]).wait()
        pack(src, raw[src, 0], raw[src, 1])

    sent = raw.at[pl.ds(0, n_s - 1)]
    pltpu.make_async_copy(sent, sent, send_a).wait()
    rest = out_ref.at[:, pl.ds(0, (n_g - 1) * cap), :]
    pltpu.make_async_copy(rest, rest, send_b).wait()
    pltpu.make_async_copy(rest, rest, recv_b).wait()


def expert_kernel(xg_ref, gate_ref, up_ref, down_ref, grad_down_ref, part_ref, total):
    step = pl.program_id(0)
    rows_in, rows_grad = xg_ref[0], xg_ref[1]
    over_features = (((1,), (1,)), ((), ()))
    gate_w, up_w, down_w = gate_ref[0], up_ref[0], down_ref[0]
    gate = lax.dot_general(rows_in, gate_w, over_features, preferred_element_type=jnp.float32)
    up = lax.dot_general(rows_in, up_w, over_features, preferred_element_type=jnp.float32)
    dhid = lax.dot_general(rows_grad, down_w, over_features, preferred_element_type=jnp.float32)
    sig = jax.nn.sigmoid(gate)
    silu = gate * sig
    hidden = (silu * up).astype(jnp.bfloat16)
    dgate = (dhid * up * sig * (1.0 + gate * (1.0 - sig))).astype(jnp.bfloat16)
    dup = (dhid * silu).astype(jnp.bfloat16)
    grad_down_ref[0] = over_rows(hidden, rows_grad).astype(jnp.bfloat16)
    term = jnp.dot(dgate, gate_w, preferred_element_type=jnp.float32) + jnp.dot(
        dup, up_w, preferred_element_type=jnp.float32
    )

    @pl.when(step == 0)
    def _():
        total[...] = term

    @pl.when(step > 0)
    def _():
        total[...] += term

    @pl.when(step == pl.num_programs(0) - 1)
    def _():
        part_ref[...] = total[...].astype(jnp.bfloat16)


def return_kernel(
    n_g, n_s, part_ref, ids_ref, out_ref, back, table, shares, got, send_a, recv_a, send_b, recv_b
):
    g, s = lax.axis_index("grp"), lax.axis_index("sl")
    count, fc = out_ref.shape
    cap = count // 2
    owners = n_g // EXPERTS
    greet(n_g, n_s)
    mine = pl.ds(pl.multiple_of(g * cap, 16), cap)

    @pl.loop(1, n_s + 1)
    def _(k):
        chunk = lax.rem(s + k, n_s)
        columns = pl.ds(pl.multiple_of(chunk * fc, 128), fc)

        @pl.loop(1, n_g)
        def _(j):
            dest = lax.rem(g + j, n_g)
            theirs = pl.ds(pl.multiple_of(dest * cap, 16), cap)
            pltpu.make_async_remote_copy(
                src_ref=part_ref.at[theirs, columns],
                dst_ref=back.at[chunk, mine, :],
                send_sem=send_a, recv_sem=recv_a.at[chunk],
                device_id=(dest, s), device_id_type=MESH,
            ).start()

        back[chunk, mine, :] = part_ref[mine, columns]

    first, second, slot0, slot1 = slots(ids_ref)
    width = n_g * cap
    table[...] = pick(first, slot0, cap, owners, width) + pick(second, slot1, cap, owners, width)

    def arrived(chunk):
        whole = back.at[chunk, pl.ds(0, (n_g - 1) * cap), :]
        pltpu.make_async_copy(whole, whole, recv_a.at[chunk]).wait()
        return jnp.dot(table[...], back[chunk], preferred_element_type=jnp.float32)

    @pl.loop(1, n_s)
    def _(k):
        chunk = lax.rem(s + k, n_s)
        shares[chunk] = arrived(chunk).astype(jnp.bfloat16)
        pltpu.make_async_remote_copy(
            src_ref=shares.at[chunk], dst_ref=got.at[s], send_sem=send_b, recv_sem=recv_b.at[s],
            device_id=(g, chunk), device_id_type=MESH,
        ).start()

    total = arrived(s)

    def add(k, total):
        src = lax.rem(s + k, n_s)
        pltpu.make_async_copy(got.at[src], got.at[src], recv_b.at[src]).wait()
        return total + got[src].astype(jnp.float32)

    total = lax.fori_loop(1, n_s, add, total)
    out_ref[...] = total.astype(jnp.bfloat16)
    sent = back.at[:, pl.ds(0, (n_g - 1) * cap), :]
    pltpu.make_async_copy(sent, sent, send_a).wait()
    shared = shares.at[pl.ds(0, n_s - 1)]
    pltpu.make_async_copy(shared, shared, send_b).wait()


def block_of(hidden):
    for size in (512, 384, 256, 192, 128):
        if hidden % size == 0:
            return size
    return hidden


def local(n_g, n_s, tokens, grad_out, expert_ids, gate_probs, gate_weight, up_weight, down_weight):
    count, fc = tokens.shape
    cap = count // 2
    rows = n_g * cap
    hidden, width = gate_weight.shape[1:]
    bf16 = jnp.bfloat16
    vmem = pl.BlockSpec(memory_space=pltpu.VMEM)
    dma = pltpu.SemaphoreType.DMA
    xg = pl.pallas_call(
        functools.partial(dispatch_kernel, n_g, n_s),
        out_shape=jax.ShapeDtypeStruct((2, rows, width), bf16),
        in_specs=[vmem] * 4,
        out_specs=vmem,
        scratch_shapes=[
            pltpu.VMEM((n_s, 2, count, fc), bf16),
            pltpu.VMEM((n_s, 2, EXPERTS * cap, fc), bf16),
            pltpu.VMEM((2, count, EXPERTS * cap), bf16),
            dma, dma((n_s,)), dma, dma,
        ],
        compiler_params=pltpu.CompilerParams(
            collective_id=0, has_side_effects=True, vmem_limit_bytes=BIG
        ),
        name="dispatch",
    )(tokens, grad_out, expert_ids, gate_probs)

    block = block_of(hidden)
    steps = hidden // block
    weight = pl.BlockSpec((1, block, width), lambda i: (0, i, 0))
    grad_down, part = pl.pallas_call(
        expert_kernel,
        grid=(steps,),
        out_shape=(
            jax.ShapeDtypeStruct((1, hidden, width), bf16),
            jax.ShapeDtypeStruct((rows, width), bf16),
        ),
        in_specs=[pl.BlockSpec((2, rows, width), lambda i: (0, 0, 0)), weight, weight, weight],
        out_specs=(weight, pl.BlockSpec((rows, width), lambda i: (0, 0))),
        scratch_shapes=[pltpu.VMEM((rows, width), jnp.float32)],
        compiler_params=pltpu.CompilerParams(
            dimension_semantics=("arbitrary",), vmem_limit_bytes=BIG
        ),
        name="experts",
    )(xg, gate_weight, up_weight, down_weight)

    grad_input = pl.pallas_call(
        functools.partial(return_kernel, n_g, n_s),
        out_shape=jax.ShapeDtypeStruct((count, fc), bf16),
        in_specs=[vmem] * 2,
        out_specs=vmem,
        scratch_shapes=[
            pltpu.VMEM((n_s, rows, fc), bf16),
            pltpu.VMEM((count, rows), bf16),
            pltpu.VMEM((n_s, count, fc), bf16),
            pltpu.VMEM((n_s, count, fc), bf16),
            dma, dma((n_s,)), dma, dma((n_s,)),
        ],
        compiler_params=pltpu.CompilerParams(
            collective_id=1, has_side_effects=True, vmem_limit_bytes=BIG
        ),
        name="give_back",
    )(part, expert_ids)
    return grad_input, grad_down


def solution(mesh):
    return jax.shard_map(
        functools.partial(local, mesh.shape["grp"], mesh.shape["sl"]),
        mesh=mesh,
        in_specs=(
            P("grp", "sl"),
            P("grp", "sl"),
            P("grp", None),
            P("grp", None),
            P("grp", "sl", None),
            P("grp", "sl", None),
            P("grp", "sl", None),
        ),
        out_specs=(P("grp", "sl"), P("grp", "sl", None)),
        check_vma=False,
    )
```

```python
import functools

import jax
import jax.numpy as jnp
from jax import lax
from jax.experimental import pallas as pl
from jax.experimental.pallas import tpu as pltpu
from jax.sharding import PartitionSpec as P

EXPERTS = 8
MESH = pl.DeviceIdType.MESH
BIG = 56 * 1024 * 1024


def greet(n_g, n_s):
    g, s = lax.axis_index("grp"), lax.axis_index("sl")
    barrier = pltpu.get_barrier_semaphore()

    @pl.loop(1, n_g)
    def _(j):
        pl.semaphore_signal(
            barrier, inc=1, device_id=(lax.rem(g + j, n_g), s), device_id_type=MESH
        )

    @pl.loop(1, n_s)
    def _(j):
        pl.semaphore_signal(
            barrier, inc=1, device_id=(g, lax.rem(s + j, n_s)), device_id_type=MESH
        )


def met(n_g, n_s):
    pl.semaphore_wait(pltpu.get_barrier_semaphore(), n_g - 1 + n_s - 1)


def upright(row):
    count = row.shape[1]
    here = lax.broadcasted_iota(jnp.int32, (count, count), 0)
    there = lax.broadcasted_iota(jnp.int32, (count, count), 1)
    return jnp.sum(jnp.where(here == there, row, jnp.zeros_like(row)), axis=1, keepdims=True)


def slots(ids_ref):
    count = ids_ref.shape[1]
    first, second = upright(ids_ref[0:1, :]), upright(ids_ref[1:2, :])
    lane = lax.broadcasted_iota(jnp.int32, (count, 128), 1)
    hit0 = (lane == first).astype(jnp.float32)
    hit1 = (lane == second).astype(jnp.float32)
    row = lax.broadcasted_iota(jnp.int32, (count, count), 0)
    col = lax.broadcasted_iota(jnp.int32, (count, count), 1)
    before = (col < row).astype(jnp.float32)
    earlier = jnp.dot(before, hit0 + hit1, preferred_element_type=jnp.float32)
    slot0 = jnp.sum(earlier * hit0, axis=1, keepdims=True).astype(jnp.int32)
    slot1 = jnp.sum(earlier * hit1, axis=1, keepdims=True).astype(jnp.int32)
    return first, second, slot0, slot1


def pick(expert, slot, cap, owners, width):
    lane = lax.broadcasted_iota(jnp.int32, (expert.shape[0], width), 1)
    table = jnp.zeros((expert.shape[0], width), jnp.float32)
    for owner in range(owners):
        table = table + (lane == (expert * owners + owner) * cap + slot).astype(jnp.float32)
    return table.astype(jnp.bfloat16)


def over_rows(left, right):
    return lax.dot_general(
        left, right, (((0,), (0,)), ((), ())), preferred_element_type=jnp.float32
    )


def dispatch_kernel(
    n_g, n_s, tok_ref, grad_ref, ids_ref, prob_ref, out_ref,
    raw, stage, table, send_a, recv_a, send_b, recv_b,
):
    g, s = lax.axis_index("grp"), lax.axis_index("sl")
    count, fc = tok_ref.shape
    cap = count // 2
    owners = n_g // EXPERTS
    greet(n_g, n_s)
    first, second, slot0, slot1 = slots(ids_ref)
    table[0] = pick(first, slot0, cap, 1, EXPERTS * cap)
    table[1] = pick(second, slot1, cap, 1, EXPERTS * cap)
    prob0, prob1 = upright(prob_ref[0:1, :]), upright(prob_ref[1:2, :])
    mine = pl.ds(pl.multiple_of(g * cap, 16), cap)

    def pack(src, tokens, grads):
        sel0, sel1 = table[0], table[1]
        wide = grads.astype(jnp.float32)
        scaled0 = (prob0 * wide).astype(jnp.bfloat16)
        scaled1 = (prob1 * wide).astype(jnp.bfloat16)
        stage[src, 0] = over_rows(sel0 + sel1, tokens).astype(jnp.bfloat16)
        stage[src, 1] = (over_rows(sel0, scaled0) + over_rows(sel1, scaled1)).astype(jnp.bfloat16)

    def send(src):
        columns = pl.ds(pl.multiple_of(src * fc, 128), fc)

        @pl.loop(1, n_g)
        def _(j):
            dest = lax.rem(g + j, n_g)
            theirs = pl.ds(pl.multiple_of((dest // owners) * cap, 16), cap)
            pltpu.make_async_remote_copy(
                src_ref=stage.at[src, :, theirs, :],
                dst_ref=out_ref.at[:, mine, columns],
                send_sem=send_b, recv_sem=recv_b,
                device_id=(dest, s), device_id_type=MESH,
            ).start()

        own = pl.ds(pl.multiple_of((g // owners) * cap, 16), cap)
        out_ref[0, mine, columns] = stage[src, 0, own, :]
        out_ref[1, mine, columns] = stage[src, 1, own, :]

    pack(s, tok_ref[...], grad_ref[...])
    met(n_g, n_s)

    @pl.loop(1, n_s)
    def _(k):
        peer = lax.rem(s + k, n_s)
        for part, ref in enumerate((tok_ref, grad_ref)):
            pltpu.make_async_remote_copy(
                src_ref=ref, dst_ref=raw.at[s, part], send_sem=send_a, recv_sem=recv_a.at[s],
                device_id=(g, peer), device_id_type=MESH,
            ).start()

    send(s)

    @pl.loop(1, n_s)
    def _(k):
        src = lax.rem(s + k, n_s)
        pltpu.make_async_copy(raw.at[src], raw.at[src], recv_a.at[src]).wait()
        pack(src, raw[src, 0], raw[src, 1])
        send(src)

    sent = raw.at[pl.ds(0, n_s - 1)]
    pltpu.make_async_copy(sent, sent, send_a).wait()
    rest = out_ref.at[:, pl.ds(0, (n_g - 1) * cap), :]
    pltpu.make_async_copy(rest, rest, send_b).wait()
    pltpu.make_async_copy(rest, rest, recv_b).wait()


def expert_kernel(xg_ref, gate_ref, up_ref, down_ref, grad_down_ref, part_ref, total):
    step = pl.program_id(0)
    rows_in, rows_grad = xg_ref[0], xg_ref[1]
    over_features = (((1,), (1,)), ((), ()))
    gate_w, up_w, down_w = gate_ref[0], up_ref[0], down_ref[0]
    gate = lax.dot_general(gate_w, rows_in, over_features, preferred_element_type=jnp.float32)
    up = lax.dot_general(up_w, rows_in, over_features, preferred_element_type=jnp.float32)
    dhid = lax.dot_general(down_w, rows_grad, over_features, preferred_element_type=jnp.float32)
    sig = jax.nn.sigmoid(gate)
    silu = gate * sig
    hidden = (silu * up).astype(jnp.bfloat16)
    dgate = (dhid * up * sig * (1.0 + gate * (1.0 - sig))).astype(jnp.bfloat16)
    dup = (dhid * silu).astype(jnp.bfloat16)
    grad_down_ref[0] = jnp.dot(hidden, rows_grad, preferred_element_type=jnp.float32).astype(
        jnp.bfloat16
    )
    term = jnp.dot(dgate.T, gate_w, preferred_element_type=jnp.float32) + jnp.dot(
        dup.T, up_w, preferred_element_type=jnp.float32
    )

    @pl.when(step == 0)
    def _():
        total[...] = term

    @pl.when(step > 0)
    def _():
        total[...] += term

    @pl.when(step == pl.num_programs(0) - 1)
    def _():
        part_ref[...] = total[...].astype(jnp.bfloat16)


def return_kernel(
    n_g, n_s, part_ref, ids_ref, out_ref, back, table, shares, got, send_a, recv_a, send_b, recv_b
):
    g, s = lax.axis_index("grp"), lax.axis_index("sl")
    count, fc = out_ref.shape
    cap = count // 2
    owners = n_g // EXPERTS
    greet(n_g, n_s)
    first, second, slot0, slot1 = slots(ids_ref)
    width = n_g * cap
    table[...] = pick(first, slot0, cap, owners, width) + pick(second, slot1, cap, owners, width)
    met(n_g, n_s)
    mine = pl.ds(pl.multiple_of(g * cap, 16), cap)

    @pl.loop(1, n_s + 1)
    def _(k):
        chunk = lax.rem(s + k, n_s)
        columns = pl.ds(pl.multiple_of(chunk * fc, 128), fc)

        @pl.loop(1, n_g)
        def _(j):
            dest = lax.rem(g + j, n_g)
            theirs = pl.ds(pl.multiple_of(dest * cap, 16), cap)
            pltpu.make_async_remote_copy(
                src_ref=part_ref.at[theirs, columns],
                dst_ref=back.at[chunk, mine, :],
                send_sem=send_a, recv_sem=recv_a.at[chunk],
                device_id=(dest, s), device_id_type=MESH,
            ).start()

        back[chunk, mine, :] = part_ref[mine, columns]

    def arrived(chunk):
        whole = back.at[chunk, pl.ds(0, (n_g - 1) * cap), :]
        pltpu.make_async_copy(whole, whole, recv_a.at[chunk]).wait()
        return jnp.dot(table[...], back[chunk], preferred_element_type=jnp.float32)

    @pl.loop(1, n_s)
    def _(k):
        chunk = lax.rem(s + k, n_s)
        shares[chunk] = arrived(chunk).astype(jnp.bfloat16)
        pltpu.make_async_remote_copy(
            src_ref=shares.at[chunk], dst_ref=got.at[s], send_sem=send_b, recv_sem=recv_b.at[s],
            device_id=(g, chunk), device_id_type=MESH,
        ).start()

    total = arrived(s)

    def add(k, total):
        src = lax.rem(s + k, n_s)
        pltpu.make_async_copy(got.at[src], got.at[src], recv_b.at[src]).wait()
        return total + got[src].astype(jnp.float32)

    total = lax.fori_loop(1, n_s, add, total)
    out_ref[...] = total.astype(jnp.bfloat16)
    sent = back.at[:, pl.ds(0, (n_g - 1) * cap), :]
    pltpu.make_async_copy(sent, sent, send_a).wait()
    shared = shares.at[pl.ds(0, n_s - 1)]
    pltpu.make_async_copy(shared, shared, send_b).wait()


def block_of(hidden):
    for size in (512, 384, 256, 192, 128):
        if hidden % size == 0:
            return size
    return hidden


def local(n_g, n_s, tokens, grad_out, expert_ids, gate_probs, gate_weight, up_weight, down_weight):
    count, fc = tokens.shape
    cap = count // 2
    rows = n_g * cap
    hidden, width = gate_weight.shape[1:]
    ids, probs = jnp.transpose(expert_ids), jnp.transpose(gate_probs)
    bf16 = jnp.bfloat16
    vmem = pl.BlockSpec(memory_space=pltpu.VMEM)
    dma = pltpu.SemaphoreType.DMA
    xg = pl.pallas_call(
        functools.partial(dispatch_kernel, n_g, n_s),
        out_shape=jax.ShapeDtypeStruct((2, rows, width), bf16),
        in_specs=[vmem] * 4,
        out_specs=vmem,
        scratch_shapes=[
            pltpu.VMEM((n_s, 2, count, fc), bf16),
            pltpu.VMEM((n_s, 2, EXPERTS * cap, fc), bf16),
            pltpu.VMEM((2, count, EXPERTS * cap), bf16),
            dma, dma((n_s,)), dma, dma,
        ],
        compiler_params=pltpu.CompilerParams(
            collective_id=0, has_side_effects=True, vmem_limit_bytes=BIG
        ),
        name="dispatch",
    )(tokens, grad_out, ids, probs)

    block = block_of(hidden)
    steps = hidden // block
    weight = pl.BlockSpec((1, block, width), lambda i: (0, i, 0))
    grad_down, part = pl.pallas_call(
        expert_kernel,
        grid=(steps,),
        out_shape=(
            jax.ShapeDtypeStruct((1, hidden, width), bf16),
            jax.ShapeDtypeStruct((rows, width), bf16),
        ),
        in_specs=[pl.BlockSpec((2, rows, width), lambda i: (0, 0, 0)), weight, weight, weight],
        out_specs=(weight, pl.BlockSpec((rows, width), lambda i: (0, 0))),
        scratch_shapes=[pltpu.VMEM((rows, width), jnp.float32)],
        compiler_params=pltpu.CompilerParams(
            dimension_semantics=("arbitrary",), vmem_limit_bytes=BIG
        ),
        name="experts",
    )(xg, gate_weight, up_weight, down_weight)

    grad_input = pl.pallas_call(
        functools.partial(return_kernel, n_g, n_s),
        out_shape=jax.ShapeDtypeStruct((count, fc), bf16),
        in_specs=[vmem] * 2,
        out_specs=vmem,
        scratch_shapes=[
            pltpu.VMEM((n_s, rows, fc), bf16),
            pltpu.VMEM((count, rows), bf16),
            pltpu.VMEM((n_s, count, fc), bf16),
            pltpu.VMEM((n_s, count, fc), bf16),
            dma, dma((n_s,)), dma, dma((n_s,)),
        ],
        compiler_params=pltpu.CompilerParams(
            collective_id=1, has_side_effects=True, vmem_limit_bytes=BIG
        ),
        name="give_back",
    )(part, ids)
    return grad_input, grad_down


def solution(mesh):
    return jax.shard_map(
        functools.partial(local, mesh.shape["grp"], mesh.shape["sl"]),
        mesh=mesh,
        in_specs=(
            P("grp", "sl"),
            P("grp", "sl"),
            P("grp", None),
            P("grp", None),
            P("grp", "sl", None),
            P("grp", "sl", None),
            P("grp", "sl", None),
        ),
        out_specs=(P("grp", "sl"), P("grp", "sl", None)),
        check_vma=False,
    )
```
